512 devices in a mesh: ctx: 32 (over z, core), head: 16 (over y, x).
Axes of the slice: x: 4, y: 4, z: 16, core: 2. Of those that a mesh axis runs over, the one named last changes fastest.
Arguments:
- q_latent: bfloat16 [4096, 65536], P('ctx', 'head'), may hold values from -8 to 8
- q_rope: bfloat16 [4096, 8192], P('ctx', 'head'), may hold values from -15 to 15
- kv_latent: bfloat16 [512, 64, 512], P('ctx'), may hold values from -6 to 6
- k_rope: bfloat16 [512, 4096], P('ctx'), may hold values from -6 to 6
- selection: int32 [64, 32], P('ctx'), may hold values from 0 to 511, as said below
- w_uv: bfloat16 [128, 512, 128], P('head'), may hold values from -0.75 to 0.75
Outputs:
- attn_out: bfloat16 [4096, 16384], P('ctx', 'head')
The draws below stay inside these ranges and needn't reach their ends.
Inputs may be any that keep to these rules, and one draw needn't show every extreme that they name: `selection`: each row lists 32 distinct blocks; block b is held by index b // 16 of ctx. The first 8 entries are the same in every row: the consecutive blocks of one tool result in increasing order, all held by one index of ctx, and no other block of that index appears in any row. Of the remaining entries of a row, at most 1 are held by any one index of ctx. For the 2 query blocks of each index of ctx (rows 2 d to 2 d + 1) there is an index of ctx from which each of them selects exactly 1 block.
All inputs are finite; a program needn't handle non-finite values.
Results may differ from the reference program's by a relative error of at most 0.0052.
Values may be sent and summed in bfloat16 or wider, within the bound.
No kernel may reach another device: no remote copies, remote signals or barrier semaphores. Data moves between devices by JAX's collectives and lax.ppermute only.
A program may use at most 64 MiB of HBM per device.

```python
import jax
import jax.numpy as jnp
from jax import lax

HEADS = 128
LAT = 512
ROPE = 64
VH = 128
BLOCK = 64
TOPK = 32
HOT = 8
BLK_DEV = 16
QB_DEV = 2
PER_OWN = 1
NBLK = 512
NQB = 64
QROWS = 4096


def tool_place(key):
    place_key = jax.random.fold_in(key, 100)
    key_one, key_two = jax.random.split(place_key)
    owners = NBLK // BLK_DEV
    hot_owner = jax.random.randint(key_one, (), 0, owners)
    hot_first = hot_owner * BLK_DEV + jax.random.randint(key_two, (), 0, BLK_DEV - HOT + 1)
    return (hot_owner, hot_first)


def draw_q_latent(key, part):
    key = jax.random.fold_in(key, 2)
    key_one = jax.random.fold_in(key, 0)
    values = jax.random.normal(key_one, (QROWS, HEADS, LAT), jnp.float32) * 1.2
    return jnp.clip(values, -8.0, 8.0).reshape(QROWS, HEADS * LAT).astype(jnp.bfloat16)


def draw_q_rope(key, part):
    key = jax.random.fold_in(key, 3)
    key_one = jax.random.fold_in(key, 0)
    values = jax.random.normal(key_one, (QROWS, HEADS, ROPE), jnp.float32) * 1.2
    values = jnp.clip(values, -8.0, 8.0)
    return values.reshape(QROWS, HEADS * ROPE).astype(jnp.bfloat16)


def draw_kv_latent(key, part):
    key = jax.random.fold_in(key, 4)
    key_one = jax.random.fold_in(key, 0)
    values = jax.random.normal(key_one, (NBLK, BLOCK, LAT), jnp.float32)
    return jnp.clip(values, -6.0, 6.0).astype(jnp.bfloat16)


def draw_k_rope(key, part):
    key = jax.random.fold_in(key, 5)
    key_one = jax.random.fold_in(key, 0)
    values = jax.random.normal(key_one, (NBLK, BLOCK, ROPE), jnp.float32)
    values = jnp.clip(values, -6.0, 6.0)
    return values.reshape(NBLK, BLOCK * ROPE).astype(jnp.bfloat16)


def draw_selection(key, part):
    hot_owner, hot_first = tool_place(key)
    key = jax.random.fold_in(key, 1)
    key_one, key_two, key_three = jax.random.split(key, 3)
    owners = NBLK // BLK_DEV
    others = owners - 1
    devices = NQB // QB_DEV
    favored = jax.random.randint(key_one, (devices,), 0, others)
    perm_keys = jax.random.split(key_two, NQB * others)

    def pick_local(one_key):
        return jax.random.permutation(one_key, BLK_DEV)[:PER_OWN]
    local_ids = jax.vmap(pick_local)(perm_keys).reshape(NQB, others, PER_OWN)
    other_owner = (hot_owner + 1 + jnp.arange(others)) % owners
    candidates = other_owner[None, :, None] * BLK_DEV + local_ids
    jitter = jax.random.randint(key_three, (NQB, others, PER_OWN), 0, 2 ** 20)
    order_ids = jnp.arange(others * PER_OWN).reshape(others, PER_OWN)
    device_of = jnp.arange(NQB) // QB_DEV
    forced = (jnp.arange(others)[None, :] == favored[device_of][:, None]).astype(jnp.int32)
    ranking = jitter * (others * PER_OWN) + order_ids[None] + forced[:, :, None] * 2 ** 28
    winners = lax.top_k(ranking.reshape(NQB, others * PER_OWN), TOPK - HOT)[1]
    cold_ids = jnp.take_along_axis(candidates.reshape(NQB, others * PER_OWN), winners, axis=1)
    hot_ids = jnp.broadcast_to(hot_first + jnp.arange(HOT), (NQB, HOT))
    return jnp.concatenate([hot_ids, cold_ids], axis=1).astype(jnp.int32)


def steps_of(rng, extent, pieces, least, high):
    gain, own = 1.0, jax.random.fold_in(rng, 6)
    for axis_at, shards_of in pieces:
        steps = jnp.exp(jax.random.uniform(jax.random.fold_in(own, axis_at), (shards_of,), jnp.float32, least / len(pieces), high / len(pieces)))
        gain = gain * jnp.repeat(steps, extent[axis_at] // shards_of).reshape([-1 if axis == axis_at else 1 for axis in range(len(extent))])
    return gain


def noise(own_key, shape, spread, reach, cuts=(), dtype=jnp.bfloat16):
    values = spread * jax.random.normal(own_key, shape, jnp.float32)
    if cuts:
        values = values * steps_of(own_key, shape, cuts, -0.22, 0.18)
    return jnp.clip(values, -reach, reach).astype(dtype)


def setup_inputs(seed: int = 0) -> dict:
    arg_keys = jax.random.split(jax.random.key(seed), 7)
    return {
        "q_latent": draw_q_latent(jax.random.fold_in(arg_keys[6], 71), 0),
        "q_rope": draw_q_rope(jax.random.fold_in(arg_keys[6], 71), 0),
        "kv_latent": draw_kv_latent(jax.random.fold_in(arg_keys[6], 71), 0),
        "k_rope": draw_k_rope(jax.random.fold_in(arg_keys[6], 71), 0),
        "selection": draw_selection(jax.random.fold_in(arg_keys[6], 71), 0),
        "w_uv": noise(arg_keys[5], (HEADS, LAT, VH), (LAT // 9) ** -0.5, 0.75, ((0, 16),)),
    }


score_scale = 192.0 ** -0.5


def reference(q_latent, q_rope, kv_latent, k_rope, selection, w_uv):
    query_latent = q_latent.reshape(NQB, BLOCK, HEADS, LAT)
    query_rope = q_rope.reshape(NQB, BLOCK, HEADS, ROPE)
    weights_uv = w_uv.astype(jnp.float32)

    def one_block(inputs):
        latents, rope_part, picked = inputs
        keys = kv_latent[picked].reshape(TOPK * BLOCK, LAT).astype(jnp.float32)
        key_rope = k_rope[picked].reshape(TOPK * BLOCK, ROPE).astype(jnp.float32)
        scores = jnp.einsum("rhc,kc->hrk", latents.astype(jnp.float32), keys)
        scores = scores + jnp.einsum("rhe,ke->hrk", rope_part.astype(jnp.float32), key_rope)
        scores = scores * score_scale
        row_max = jnp.max(scores, axis=2, keepdims=True)
        weights = jnp.exp(scores - row_max)
        row_total = jnp.sum(weights, axis=2)
        probs = lax.optimization_barrier(weights.astype(jnp.bfloat16)).astype(jnp.float32)
        blended = jnp.einsum("hrk,kc->hrc", probs, keys)
        latent_out = (blended / row_total[:, :, None]).astype(jnp.bfloat16)
        latent_out = lax.optimization_barrier(latent_out).astype(jnp.float32)
        projected = jnp.einsum("hrc,hcv->rhv", latent_out, weights_uv)
        return projected.reshape(BLOCK, HEADS * VH).astype(jnp.bfloat16)

    results = lax.map(one_block, (query_latent, query_rope, selection))
    return results.reshape(QROWS, HEADS * VH)
```

```python
import jax
import jax.numpy as jnp
from jax import lax
from jax.experimental import pallas as pl
from jax.experimental.pallas import tpu as pltpu
from jax.sharding import Mesh
from jax.sharding import PartitionSpec as P

LAT = 512
ROPE = 64
VH = 128
HOT = 8
WIDE = 640
SHARE = 8
QB = 64
HEADS = 8

SCORE_SCALE = 192.0 ** (-0.5)
LOG2E = 1.4426950408889634
VMEM_LIMIT = 56 * 1024 * 1024

bf16 = jnp.bfloat16
f32 = jnp.float32


def pick_kernel(index_ref, blocks_ref, hot_ref, out_ref):
    hot = hot_ref[...]
    for z in range(16):
        for c in range(2):
            out_ref[z, c] = blocks_ref[index_ref[z * 2 + c]]
        out_ref[z, 2] = hot


def compact_kernel(index_ref, got_ref, out_ref):
    for i in range(24):
        slot = index_ref[i]
        out_ref[i * 8 : i * 8 + 8, :] = got_ref[slot // 2, slot % 2]
    for i in range(8):
        out_ref[192 + i * 8 : 200 + i * 8, :] = jnp.concatenate(
            [got_ref[2 * i, 2, 0:4], got_ref[2 * i + 1, 2, 0:4]], axis=0
        )


def attend_kernel(q0_ref, q1_ref, mine_ref, other_ref, w0_ref, w1_ref, o0_ref, o1_ref, q_scr):
    zeros = jnp.zeros((QB, WIDE - LAT - ROPE), bf16)
    for r, q_ref in enumerate((q0_ref, q1_ref)):
        for h in range(HEADS):
            base = HEADS * LAT + h * ROPE
            rows = pl.ds((r * HEADS + h) * QB, QB)
            q_scr[rows, 0:LAT] = q_ref[:, h * LAT : (h + 1) * LAT]
            q_scr[rows, LAT:WIDE] = jnp.concatenate([q_ref[:, base : base + ROPE], zeros], axis=1)

    for r, (w_ref, o_ref) in enumerate(((w0_ref, o0_ref), (w1_ref, o1_ref))):
        for part in range(2):
            q = q_scr[(r * 2 + part) * 256 : (r * 2 + part + 1) * 256, :]
            scores = []
            for ref in (mine_ref, other_ref):
                for i in range(4):
                    scores.append(
                        lax.dot_general(
                            q, ref[i], (((1,), (1,)), ((), ())), preferred_element_type=f32
                        )
                    )
            top = scores[0]
            for s in scores[1:]:
                top = jnp.maximum(top, s)
            top = jnp.max(top, axis=1, keepdims=True) * (SCORE_SCALE * LOG2E)
            blended = jnp.zeros((256, LAT), f32)
            total = jnp.zeros((256, 256), f32)
            for n, ref in enumerate((mine_ref, other_ref)):
                for i in range(4):
                    w = jnp.exp2(scores[n * 4 + i] * (SCORE_SCALE * LOG2E) - top)
                    total = total + w
                    blended = blended + jnp.dot(
                        w.astype(bf16), ref[i, :, 0:LAT], preferred_element_type=f32
                    )
            total = jnp.sum(total, axis=1, keepdims=True)
            latent = (blended / total).astype(bf16)
            for n in range(4):
                h = part * 4 + n
                o_ref[:, h * VH : (h + 1) * VH] = jnp.dot(
                    latent[n * QB : (n + 1) * QB], w_ref[h], preferred_element_type=f32
                ).astype(bf16)


def local(q_latent, q_rope, kv_latent, k_rope, selection, w_uv):
    z, k, y, x = (lax.axis_index(a) for a in ("z", "core", "y", "x"))
    vmem = pl.BlockSpec(memory_space=pltpu.VMEM)
    smem = pl.BlockSpec(memory_space=pltpu.SMEM)

    def pairs(r):
        return [
            (c * 4 + s, (s // 2) * 4 + 2 * c + (s + r) % 2) for c in range(2) for s in range(4)
        ]

    queries, ups = [], []
    for r in range(2):
        m = (x + r) % 2
        part = jnp.concatenate(
            [
                lax.dynamic_slice_in_dim(q_latent, m * QB, QB, 0),
                lax.dynamic_slice_in_dim(q_rope, m * QB, QB, 0),
            ],
            axis=1,
        )
        queries.append(lax.ppermute(part, ("core", "x"), pairs(r)))
    for r in range(2):
        ups.append(lax.ppermute(w_uv, ("core", "x"), pairs(r)))

    lat = lax.dynamic_slice_in_dim(kv_latent, y * 16, 16, 1)
    rope = lax.dynamic_slice_in_dim(k_rope, y * 1024, 1024, 1).reshape(16, 16, ROPE)
    share = jnp.concatenate([lat, rope, jnp.zeros((16, 16, WIDE - LAT - ROPE), bf16)], axis=2)
    own = lax.dynamic_slice_in_dim(share, k * SHARE, SHARE, 1)
    theirs = lax.dynamic_slice_in_dim(share, (1 - k) * SHARE, SHARE, 1)
    swapped = lax.ppermute(theirs, "core", [(0, 1), (1, 0)])
    blocks = jnp.where(k == 0, jnp.stack([own, swapped]), jnp.stack([swapped, own]))
    blocks = blocks.reshape(32, SHARE, WIDE)

    hot_first = selection[0, 0]
    hot_owner = hot_first // 16
    hot = lax.dynamic_slice_in_dim(share, hot_first - hot_owner * 16, HOT, 0)
    hot = hot.reshape(8, 2, 2, 4, WIDE).transpose(0, 2, 1, 3, 4).reshape(32, 4, WIDE)
    cold = selection[:, HOT:]
    owner = cold // 16
    place = cold - owner * 16 + 1
    match = owner[:, :, None] == jnp.arange(32)[None, None, :]
    wants = jnp.sum(jnp.where(match, place[:, :, None], 0), axis=1)
    wants = wants.reshape(2, 16, 2).transpose(1, 0, 2).reshape(16, 1, 4)
    wants = jnp.broadcast_to(wants, (16, 2, 4)).reshape(32, 4)
    notes = jnp.concatenate(
        [
            wants,
            jnp.broadcast_to(owner.reshape(1, 48), (32, 48)),
            jnp.zeros((32, 76), jnp.int32),
        ],
        axis=1,
    ).astype(bf16)
    first = jnp.concatenate(
        [
            hot[:, :, :LAT].reshape(32, 16, 128),
            hot[:, :, LAT : LAT + ROPE].reshape(32, 2, 128),
            notes[:, None, :],
            jnp.zeros((32, 5, 128), bf16),
        ],
        axis=1,
    )
    first = lax.all_to_all(first, ("z", "core"), split_axis=0, concat_axis=0, tiled=True)

    relay = lax.dynamic_index_in_dim(first, hot_owner, 0, keepdims=False)
    relay = jnp.concatenate(
        [
            relay[:16].reshape(4, LAT),
            relay[16:18].reshape(4, ROPE),
            jnp.zeros((4, WIDE - LAT - ROPE), bf16),
        ],
        axis=1,
    )
    relay = jnp.concatenate([relay, relay], axis=0)
    notes = first[:, 18, :].reshape(16, 2, 128)
    notes = lax.dynamic_index_in_dim(notes, x // 2, 1, keepdims=False)
    wants = lax.dynamic_slice_in_dim(notes, (x % 2) * 2, 2, 1).astype(jnp.int32)
    wants = jnp.maximum(wants - 1, 0) + jnp.arange(2)[None, :] * 16
    owners = lax.dynamic_index_in_dim(notes, z, 0, keepdims=False)
    owners = lax.dynamic_slice_in_dim(owners, 4 + (x % 2) * 24, 24, 0).astype(jnp.int32)

    second = pl.pallas_call(
        pick_kernel,
        out_shape=jax.ShapeDtypeStruct((16, 3, SHARE, WIDE), bf16),
        in_specs=[smem, vmem, vmem],
        out_specs=vmem,
    )(wants.reshape(32), blocks, relay)
    second = lax.all_to_all(second, "z", split_axis=0, concat_axis=0, tiled=True)

    keys = pl.pallas_call(
        compact_kernel,
        out_shape=jax.ShapeDtypeStruct((256, WIDE), bf16),
        in_specs=[smem, vmem],
        out_specs=vmem,
    )(owners, second)
    keys = jnp.broadcast_to(keys[None], (4, 256, WIDE))
    keys = lax.all_to_all(keys, "y", split_axis=0, concat_axis=0, tiled=True)
    other = lax.ppermute(keys, "core", [(0, 1), (1, 0)])

    out = jax.ShapeDtypeStruct((QB, HEADS * VH), bf16)
    outs = pl.pallas_call(
        attend_kernel,
        out_shape=[out, out],
        in_specs=[vmem] * 6,
        out_specs=[vmem] * 2,
        scratch_shapes=[pltpu.VMEM((2 * HEADS * QB, WIDE), bf16)],
        compiler_params=pltpu.CompilerParams(vmem_limit_bytes=VMEM_LIMIT),
    )(queries[0], queries[1], keys, other, ups[0], ups[1])

    back = [
        lax.ppermute(outs[r], ("core", "x"), [(d, s) for s, d in pairs(r)]) for r in range(2)
    ]
    even = x % 2 == 0
    return jnp.concatenate(
        [jnp.where(even, back[0], back[1]), jnp.where(even, back[1], back[0])], axis=0
    )


def solution(mesh):
    grid = Mesh(mesh.devices.reshape(16, 2, 4, 4), ("z", "core", "y", "x"))
    ctx, head = ("z", "core"), ("y", "x")
    in_specs = (
        P(ctx, head),
        P(ctx, head),
        P(ctx, None, None),
        P(ctx, None),
        P(ctx, None),
        P(head, None, None),
    )
    return jax.shard_map(
        local, mesh=grid, in_specs=in_specs, out_specs=P(ctx, head), check_vma=False
    )
```

```python
import jax
import jax.numpy as jnp
from jax import lax
from jax.experimental import pallas as pl
from jax.experimental.pallas import tpu as pltpu
from jax.sharding import Mesh
from jax.sharding import PartitionSpec as P

LAT = 512
ROPE = 64
VH = 128
HOT = 8
WIDE = 640
SHARE = 8
QB = 64
HEADS = 8

SCORE_SCALE = 192.0 ** (-0.5)
LOG2E = 1.4426950408889634
VMEM_LIMIT = 56 * 1024 * 1024

bf16 = jnp.bfloat16
f32 = jnp.float32


def pick_kernel(index_ref, blocks_ref, hot_ref, out_ref):
    hot = hot_ref[...]
    for z in range(16):
        for c in range(2):
            out_ref[z, c] = blocks_ref[index_ref[z * 2 + c]]
        out_ref[z, 2] = hot


def compact_kernel(index_ref, got_ref, out_ref):
    for i in range(24):
        slot = index_ref[i]
        out_ref[i * 8 : i * 8 + 8, :] = got_ref[slot // 2, slot % 2]
    for i in range(8):
        out_ref[192 + i * 8 : 200 + i * 8, :] = jnp.concatenate(
            [got_ref[2 * i, 2, 0:4], got_ref[2 * i + 1, 2, 0:4]], axis=0
        )


def layout_kernel(q_ref, out_ref):
    zeros = jnp.zeros((QB, WIDE - LAT - ROPE), bf16)
    for h in range(HEADS):
        base = HEADS * LAT + h * ROPE
        rows = pl.ds(h * QB, QB)
        out_ref[rows, 0:LAT] = q_ref[:, h * LAT : (h + 1) * LAT]
        out_ref[rows, LAT:WIDE] = jnp.concatenate([q_ref[:, base : base + ROPE], zeros], axis=1)


def attend_kernel(q_ref, *refs):
    pieces, w_ref, o_ref = refs[:8], refs[8], refs[9]
    q = q_ref[...]
    scores = [
        lax.dot_general(q, piece[...], (((1,), (1,)), ((), ())), preferred_element_type=f32)
        for piece in pieces
    ]
    top = scores[0]
    for s in scores[1:]:
        top = jnp.maximum(top, s)
    top = jnp.max(top, axis=1, keepdims=True) * (SCORE_SCALE * LOG2E)
    blended = jnp.zeros((HEADS * QB, LAT), f32)
    total = jnp.zeros((HEADS * QB, 256), f32)
    for s, piece in zip(scores, pieces):
        w = jnp.exp2(s * (SCORE_SCALE * LOG2E) - top)
        total = total + w
        blended = blended + jnp.dot(w.astype(bf16), piece[:, 0:LAT], preferred_element_type=f32)
    total = jnp.sum(total, axis=1, keepdims=True)
    latent = (blended / total).astype(bf16)
    for h in range(HEADS):
        o_ref[:, h * VH : (h + 1) * VH] = jnp.dot(
            latent[h * QB : (h + 1) * QB], w_ref[h], preferred_element_type=f32
        ).astype(bf16)


def local(q_latent, q_rope, kv_latent, k_rope, selection, w_uv):
    z, k, y, x = (lax.axis_index(a) for a in ("z", "core", "y", "x"))
    vmem = pl.BlockSpec(memory_space=pltpu.VMEM)
    smem = pl.BlockSpec(memory_space=pltpu.SMEM)
    params = pltpu.CompilerParams(vmem_limit_bytes=VMEM_LIMIT)
    swap = [(0, 1), (1, 0)]

    def pairs(r):
        return [
            (c * 4 + s, (s // 2) * 4 + 2 * c + (s + r) % 2) for c in range(2) for s in range(4)
        ]

    queries, ups = [], []
    for r in range(2):
        m = (x + r) % 2
        part = jnp.concatenate(
            [
                lax.dynamic_slice_in_dim(q_latent, m * QB, QB, 0),
                lax.dynamic_slice_in_dim(q_rope, m * QB, QB, 0),
            ],
            axis=1,
        )
        queries.append(lax.ppermute(part, ("core", "x"), pairs(r)))
    for r in range(2):
        ups.append(lax.ppermute(w_uv, ("core", "x"), pairs(r)))

    lat = lax.dynamic_slice_in_dim(kv_latent, y * 16, 16, 1)
    rope = lax.dynamic_slice_in_dim(k_rope, y * 1024, 1024, 1).reshape(16, 16, ROPE)
    share = jnp.concatenate([lat, rope, jnp.zeros((16, 16, WIDE - LAT - ROPE), bf16)], axis=2)
    own = lax.dynamic_slice_in_dim(share, k * SHARE, SHARE, 1)
    theirs = lax.dynamic_slice_in_dim(share, (1 - k) * SHARE, SHARE, 1)
    hot_first = jnp.max(selection[:, 0])
    cold = selection[:, HOT:]
    notes = jnp.concatenate([cold >> 4, cold & 15], axis=1).astype(bf16)
    notes = jnp.pad(notes, ((0, 6), (0, WIDE - 48)))
    swapped = lax.ppermute(jnp.concatenate([theirs, notes[None]], axis=0), "core", swap)
    blocks = jnp.where(
        k == 0, jnp.concatenate([own, swapped[:16]]), jnp.concatenate([swapped[:16], own])
    )
    notes = jnp.where(x // 2 == k, notes, swapped[16])
    notes = jnp.where(x % 2 == 0, notes[0, :48], notes[1, :48]).astype(jnp.int32)
    owners, places = notes[:24], notes[24:]

    match = owners[None, :] == jnp.arange(32)[:, None]
    wants = jnp.sum(jnp.where(match, places[None, :], 0), axis=1).reshape(16, 1, 2)
    hot = lax.dynamic_slice_in_dim(blocks, hot_first & 31, HOT, 0).reshape(16, 4, WIDE)
    first = jnp.concatenate(
        [
            hot[:, :, :LAT].reshape(16, 16, 128),
            hot[:, :, LAT : LAT + ROPE].reshape(16, 2, 128),
            jnp.pad(wants.astype(bf16), ((0, 0), (0, 5), (0, 126))),
        ],
        axis=1,
    )
    first = lax.all_to_all(first, "z", split_axis=0, concat_axis=0, tiled=True)
    first, ups[0] = lax.optimization_barrier((first, ups[0]))

    relay = lax.dynamic_index_in_dim(first, hot_first >> 5, 0, keepdims=False)
    relay = jnp.concatenate(
        [
            relay[:16].reshape(4, LAT),
            relay[16:18].reshape(4, ROPE),
            jnp.zeros((4, WIDE - LAT - ROPE), bf16),
        ],
        axis=1,
    )
    relay = jnp.concatenate([relay, relay], axis=0)
    wants = first[:, 18, 0:2].astype(jnp.int32) + jnp.arange(2)[None, :] * 16

    second = pl.pallas_call(
        pick_kernel,
        out_shape=jax.ShapeDtypeStruct((16, 3, SHARE, WIDE), bf16),
        in_specs=[smem, vmem, vmem],
        out_specs=vmem,
    )(wants.reshape(32), blocks, relay)
    second = lax.all_to_all(second, "z", split_axis=0, concat_axis=0, tiled=True)
    second, queries, ups[1] = lax.optimization_barrier((second, queries, ups[1]))

    mine = pl.pallas_call(
        compact_kernel,
        out_shape=jax.ShapeDtypeStruct((256, WIDE), bf16),
        in_specs=[smem, vmem],
        out_specs=vmem,
    )(owners, second)
    keys = [mine]
    for step in (1, 3, 2):
        keys.append(lax.ppermute(mine, "y", [(i, (i + step) % 4) for i in range(4)]))
    keys = keys + [lax.ppermute(piece, "core", swap) for piece in keys]

    outs = []
    for r in range(2):
        q = pl.pallas_call(
            layout_kernel,
            out_shape=jax.ShapeDtypeStruct((HEADS * QB, WIDE), bf16),
            in_specs=[vmem],
            out_specs=vmem,
        )(queries[r])
        out = pl.pallas_call(
            attend_kernel,
            out_shape=jax.ShapeDtypeStruct((QB, HEADS * VH), bf16),
            in_specs=[vmem] * 10,
            out_specs=vmem,
            compiler_params=params,
        )(q, *keys, ups[r])
        outs.append(lax.ppermute(out, ("core", "x"), [(d, s) for s, d in pairs(r)]))
    even = x % 2 == 0
    return jnp.concatenate(
        [jnp.where(even, outs[0], outs[1]), jnp.where(even, outs[1], outs[0])], axis=0
    )


def solution(mesh):
    grid = Mesh(mesh.devices.reshape(16, 2, 4, 4), ("z", "core", "y", "x"))
    ctx, head = ("z", "core"), ("y", "x")
    in_specs = (
        P(ctx, head),
        P(ctx, head),
        P(ctx, None, None),
        P(ctx, None),
        P(ctx, None),
        P(head, None, None),
    )
    return jax.shard_map(
        local, mesh=grid, in_specs=in_specs, out_specs=P(ctx, head), check_vma=False
    )
```

```python
import jax
import jax.numpy as jnp
from jax import lax
from jax.experimental import pallas as pl
from jax.experimental.pallas import tpu as pltpu
from jax.sharding import Mesh
from jax.sharding import PartitionSpec as P

LAT = 512
ROPE = 64
VH = 128
HOT = 8
COLD = 24
WIDE = LAT + 2 * ROPE
SHARE = 8
QB = 64
HEADS = 8
PACK = 24
ROWS = 288

SCORE_SCALE = 192.0 ** (-0.5)
LOG2E = 1.4426950408889634

bf16 = jnp.bfloat16
f32 = jnp.float32
i32 = jnp.int32


def iota(shape, axis):
    return lax.broadcasted_iota(i32, shape, axis)


def one_hot(index, width):
    return jnp.where(index == iota((index.shape[0], width), 1), 1.0, 0.0).astype(bf16)


def pick(selector, rows):
    return jnp.dot(selector, rows, preferred_element_type=f32)


def send_kernel(hot_ref, first_ref, lat_ref, rope_ref, out_ref):
    got = first_ref[...].reshape(16 * 8, LAT)
    row = iota((256, 1), 0)
    notes = pick(one_hot(row // 16 * 8 + 5, 128), got[:, 0:128])
    lane = iota((256, 128), 1)
    want = jnp.sum(jnp.where(lane == row // 8 % 2, notes, 0.0), axis=1, keepdims=True)
    lat = pick(one_hot(want.astype(i32) * 8 + row % 8, 256), lat_ref[...].reshape(256, LAT))
    row = iota((128, 1), 0)
    notes = pick(one_hot(row // 8 * 8 + 5, 128), got[:, 0:128])
    lane = iota((128, 128), 1)
    want = jnp.sum(jnp.where(lane == row % 8, notes, 0.0), axis=1, keepdims=True).astype(i32)
    want = jnp.where(row % 8 < 2, want, -1)
    rope = pick(one_hot(want, 32), rope_ref[...])
    row = iota((8, 1), 0)
    source = jnp.where(row == 2, 4, jnp.where(row >= 4, row - 4, -1))
    hot = pick(one_hot(hot_ref[0] * 8 + source, 128) * (source >= 0).astype(bf16), got)
    for z in range(16):
        out_ref[z, 0:16, :] = lat[z * 16 : z * 16 + 16].astype(bf16)
        out_ref[z, 16:24, :] = (rope[z * 8 : z * 8 + 8] + hot).astype(bf16)


def share_kernel(owners_ref, got_ref, out_ref, got, rows, sems):
    copy = pltpu.make_async_copy(got_ref, got, sems.at[0])
    copy.start()
    row = iota((256, 1), 0)
    slot, token = row % 32, row // 32
    index = (slot - COLD) * (2 * PACK) + token // 4 * PACK + 20 + token % 4
    rope_slot = iota((32, 1), 0)
    rope_index = (rope_slot - COLD) * (2 * PACK) + 18
    for i in range(COLD):
        owner = owners_ref[i]
        at, side = owner // 2 * PACK, owner % 2
        index = jnp.where(slot == i, at + side * SHARE + token, index)
        rope_index = jnp.where(rope_slot == i, at + 16 + side, rope_index)
    lat = one_hot(index, 16 * PACK)
    rope = one_hot(rope_index, 16 * PACK)
    copy.wait()
    table = got[...].reshape(16 * PACK, LAT)
    rows[0:256, :] = pick(lat, table).astype(bf16)
    rows[256:ROWS, :] = pick(rope, table).astype(bf16)
    copies = [pltpu.make_async_copy(rows, out_ref.at[n], sems.at[n]) for n in range(4)]
    for copy in copies:
        copy.start()
    for copy in copies:
        copy.wait()


def layout_kernel(q_ref, out_ref, q, sem):
    copy = pltpu.make_async_copy(q_ref, q, sem)
    copy.start()
    copy.wait()
    for h in range(HEADS):
        base = HEADS * LAT + h * ROPE
        rows = pl.ds(h * QB, QB)
        part = q[:, base : base + ROPE]
        out_ref[rows, 0:LAT] = q[:, h * LAT : (h + 1) * LAT]
        out_ref[rows, LAT:WIDE] = jnp.concatenate([part, part], axis=1)


def bring(ref, keys, ropes, sems):
    copies = []
    for n in range(4):
        copies.append(pltpu.make_async_copy(ref.at[n, 0:256], keys.at[n], sems.at[n]))
        copies.append(pltpu.make_async_copy(ref.at[n, 256:ROWS], ropes.at[n], sems.at[4 + n]))
    for copy in copies:
        copy.start()
    return copies


def spread(ropes, places):
    lane = iota((32, 2 * ROPE), 1)
    for n in range(4):
        for t in range(SHARE):
            pair = ropes[n, :, t // 2 * 128 : t // 2 * 128 + 128]
            own = lane < ROPE if t % 2 == 0 else lane >= ROPE
            places[n, t * 32 : t * 32 + 32, :] = jnp.where(own, pair, 0)


def attend(q_ref, keys, places):
    scores = []
    for n in range(4):
        scores.append(
            lax.dot_general(
                q_ref[...],
                jnp.concatenate([keys[n], places[n]], axis=1),
                (((1,), (1,)), ((), ())),
                preferred_element_type=f32,
            )
        )
    top = jnp.maximum(jnp.maximum(scores[0], scores[1]), jnp.maximum(scores[2], scores[3]))
    top = jnp.max(top, axis=1, keepdims=True) * (SCORE_SCALE * LOG2E)
    total = jnp.zeros((HEADS * QB, 256), f32)
    blended = jnp.zeros((HEADS * QB, LAT), f32)
    for n, s in enumerate(scores):
        p = jnp.exp2(s * (SCORE_SCALE * LOG2E) - top)
        total = total + p
        blended = blended + jnp.dot(p.astype(bf16), keys[n], preferred_element_type=f32)
    return top, jnp.sum(total, axis=1, keepdims=True), blended


def first_half_kernel(
    q0_ref, q1_ref, mine_ref, blend0_ref, stat0_ref, blend1_ref, stat1_ref, keys, ropes, places, sems
):
    copies = bring(mine_ref, keys, ropes, sems)
    for copy in copies:
        copy.wait()
    spread(ropes, places)
    outs = ((q0_ref, blend0_ref, stat0_ref), (q1_ref, blend1_ref, stat1_ref))
    for q_ref, blend_ref, stat_ref in outs:
        top, total, blended = attend(q_ref, keys, places)
        blend_ref[...] = blended
        stat_ref[:, 0:128] = jnp.broadcast_to(top, (HEADS * QB, 128))
        stat_ref[:, 128:256] = jnp.broadcast_to(total, (HEADS * QB, 128))


def second_half_kernel(
    q_ref, other_ref, blend_ref, stat_ref, w_ref, o_ref, keys, ropes, places, w, sems
):
    copies = bring(other_ref, keys, ropes, sems)
    up = pltpu.make_async_copy(w_ref, w, sems.at[8])
    up.start()
    for copy in copies:
        copy.wait()
    spread(ropes, places)
    top, total, blended = attend(q_ref, keys, places)
    top0, total0 = stat_ref[:, 0:1], stat_ref[:, 128:129]
    both = jnp.maximum(top, top0)
    mine, other = jnp.exp2(top0 - both), jnp.exp2(top - both)
    scale = 1.0 / (total0 * mine + total * other)
    latent = (blend_ref[...] * (mine * scale) + blended * (other * scale)).astype(bf16)
    up.wait()
    for h in range(HEADS):
        o_ref[:, h * VH : (h + 1) * VH] = jnp.dot(
            latent[h * QB : (h + 1) * QB], w[h], preferred_element_type=f32
        ).astype(bf16)


def local(q_latent, q_rope, kv_latent, k_rope, selection, w_uv):
    z, k, y, x = (lax.axis_index(a) for a in ("z", "core", "y", "x"))
    vmem = pl.BlockSpec(memory_space=pltpu.VMEM)
    smem = pl.BlockSpec(memory_space=pltpu.SMEM)
    anywhere = pl.BlockSpec(memory_space=pl.ANY)
    swap = [(0, 1), (1, 0)]

    lat = lax.dynamic_slice_in_dim(kv_latent, y * 16, 16, 1)
    rope = lax.dynamic_slice_in_dim(k_rope, y * 1024, 1024, 1)
    hot_first = jnp.max(selection[:, 0])
    cold = selection[:, HOT:]
    notes = jnp.concatenate([cold >> 4, cold & 15], axis=1).astype(bf16)
    notes = jnp.pad(notes, ((0, 6), (0, LAT - 2 * COLD)))
    theirs = jnp.concatenate(
        [
            lax.dynamic_slice_in_dim(lat, (1 - k) * SHARE, SHARE, 1).reshape(128, LAT),
            lax.dynamic_slice_in_dim(rope, (1 - k) * LAT, LAT, 1),
            notes,
        ],
        axis=0,
    )
    swapped = lax.ppermute(theirs, "core", swap)
    own = lax.dynamic_slice_in_dim(lat, k * SHARE, SHARE, 1)
    other = swapped[:128].reshape(16, SHARE, LAT)
    lat = jnp.where(k == 0, jnp.concatenate([own, other]), jnp.concatenate([other, own]))
    own, other = lax.dynamic_slice_in_dim(rope, k * LAT, LAT, 1), swapped[128:144]
    rope = jnp.where(k == 0, jnp.concatenate([own, other]), jnp.concatenate([other, own]))
    notes = jnp.where(x // 2 == k, notes, swapped[144:])
    notes = jnp.where(x % 2 == 0, notes[0, : 2 * COLD], notes[1, : 2 * COLD]).astype(i32)
    owners, places = notes[:COLD], notes[COLD:]

    match = owners[None, :] == jnp.arange(32)[:, None]
    wants = jnp.sum(jnp.where(match, places[None, :], 0), axis=1).reshape(16, 2)
    wants = wants + jnp.arange(2)[None, :] * 16
    hot = lax.dynamic_slice_in_dim(lat, hot_first & 31, HOT, 0).reshape(16, 4, LAT)
    hot_rope = lax.dynamic_slice_in_dim(rope, hot_first & 31, HOT, 0)
    hot_rope = jnp.broadcast_to(hot_rope[:, None, None, :], (HOT, 2, 1, LAT)).reshape(16, 1, LAT)
    wants = jnp.pad(wants.astype(bf16)[:, None, :], ((0, 0), (0, 2), (0, LAT - 2)))
    first = jnp.concatenate([hot, hot_rope, wants], axis=1)
    first, w_later = lax.optimization_barrier((first, w_uv))
    first = lax.all_to_all(first, "z", split_axis=0, concat_axis=0, tiled=True)

    def pairs(r):
        return [
            (c * 4 + s, (s // 2) * 4 + 2 * c + (s + r) % 2) for c in range(2) for s in range(4)
        ]

    ups = [lax.ppermute(w, ("core", "x"), pairs(r)) for r, w in enumerate((w_uv, w_later))]
    first, ups[0] = lax.optimization_barrier((first, ups[0]))
    queries = []
    for r in range(2):
        m = (x + r) % 2
        part = jnp.concatenate(
            [
                lax.dynamic_slice_in_dim(q_latent, m * QB, QB, 0),
                lax.dynamic_slice_in_dim(q_rope, m * QB, QB, 0),
            ],
            axis=1,
        )
        queries.append(lax.ppermute(part, ("core", "x"), pairs(r)))

    second = pl.pallas_call(
        send_kernel,
        out_shape=jax.ShapeDtypeStruct((16, PACK, LAT), bf16),
        in_specs=[smem, vmem, vmem, vmem],
        out_specs=vmem,
    )((hot_first >> 5)[None], first, lat, rope)
    second = lax.all_to_all(second, "z", split_axis=0, concat_axis=0, tiled=True)
    second, queries = lax.optimization_barrier((second, queries))

    keys = pl.pallas_call(
        share_kernel,
        out_shape=jax.ShapeDtypeStruct((4, ROWS, LAT), bf16),
        in_specs=[smem, anywhere],
        out_specs=anywhere,
        scratch_shapes=[
            pltpu.VMEM((16, PACK, LAT), bf16),
            pltpu.VMEM((ROWS, LAT), bf16),
            pltpu.SemaphoreType.DMA((4,)),
        ],
    )(owners, second)
    queries = [
        pl.pallas_call(
            layout_kernel,
            out_shape=jax.ShapeDtypeStruct((HEADS * QB, WIDE), bf16),
            in_specs=[anywhere],
            out_specs=vmem,
            scratch_shapes=[
                pltpu.VMEM((QB, HEADS * (LAT + ROPE)), bf16),
                pltpu.SemaphoreType.DMA,
            ],
        )(q)
        for q in queries
    ]
    mine = lax.all_to_all(keys, "y", split_axis=0, concat_axis=0, tiled=True)
    mine, queries, ups[1] = lax.optimization_barrier((mine, queries, ups[1]))
    other = lax.ppermute(mine, "core", swap)

    rows = HEADS * QB
    blend = jax.ShapeDtypeStruct((rows, LAT), f32)
    stat = jax.ShapeDtypeStruct((rows, 256), f32)
    scratch = [
        pltpu.VMEM((4, 256, LAT), bf16),
        pltpu.VMEM((4, 32, LAT), bf16),
        pltpu.VMEM((4, 256, 2 * ROPE), bf16),
    ]
    params = pltpu.CompilerParams(vmem_limit_bytes=24 * 1024 * 1024)
    halves = pl.pallas_call(
        first_half_kernel,
        out_shape=[blend, stat, blend, stat],
        in_specs=[vmem, vmem, anywhere],
        out_specs=[vmem] * 4,
        scratch_shapes=scratch + [pltpu.SemaphoreType.DMA((8,))],
        compiler_params=params,
    )(queries[0], queries[1], mine)
    outs = []
    for r in range(2):
        out = pl.pallas_call(
            second_half_kernel,
            out_shape=jax.ShapeDtypeStruct((QB, HEADS * VH), bf16),
            in_specs=[vmem, anywhere, vmem, vmem, anywhere],
            out_specs=vmem,
            scratch_shapes=scratch
            + [pltpu.VMEM((HEADS, LAT, VH), bf16), pltpu.SemaphoreType.DMA((9,))],
            compiler_params=params,
        )(queries[r], other, halves[2 * r], halves[2 * r + 1], ups[r])
        outs.append(lax.ppermute(out, ("core", "x"), [(d, s) for s, d in pairs(r)]))
    even = x % 2 == 0
    return jnp.concatenate(
        [jnp.where(even, outs[0], outs[1]), jnp.where(even, outs[1], outs[0])], axis=0
    )


def solution(mesh):
    grid = Mesh(mesh.devices.reshape(16, 2, 4, 4), ("z", "core", "y", "x"))
    ctx, head = ("z", "core"), ("y", "x")
    in_specs = (
        P(ctx, head),
        P(ctx, head),
        P(ctx, None, None),
        P(ctx, None),
        P(ctx, None),
        P(head, None, None),
    )
    return jax.shard_map(
        local, mesh=grid, in_specs=in_specs, out_specs=P(ctx, head), check_vma=False
    )
```

```python
import jax
import jax.numpy as jnp
from jax import lax
from jax.experimental import pallas as pl
from jax.experimental.pallas import tpu as pltpu
from jax.sharding import Mesh
from jax.sharding import PartitionSpec as P

LAT = 512
ROPE = 64
VH = 128
HOT = 8
COLD = 24
WIDE = LAT + 2 * ROPE
SHARE = 8
QB = 64
HEADS = 8
PACK = 24
ROWS = 288

SCORE_SCALE = 192.0 ** (-0.5)
LOG2E = 1.4426950408889634

bf16 = jnp.bfloat16
f32 = jnp.float32
i32 = jnp.int32


def iota(shape, axis):
    return lax.broadcasted_iota(i32, shape, axis)


def one_hot(index, width):
    return jnp.where(index == iota((index.shape[0], width), 1), 1.0, 0.0).astype(bf16)


def pick(selector, rows):
    return jnp.dot(selector, rows, preferred_element_type=f32)


def send_kernel(hot_ref, first_ref, lat_ref, rope_ref, out_ref):
    got = first_ref[...].reshape(16 * 8, LAT)
    row = iota((256, 1), 0)
    notes = pick(one_hot(row // 16 * 8 + 5, 128), got[:, 0:128])
    lane = iota((256, 128), 1)
    want = jnp.sum(jnp.where(lane == row // 8 % 2, notes, 0.0), axis=1, keepdims=True)
    lat = pick(one_hot(want.astype(i32) * 8 + row % 8, 256), lat_ref[...].reshape(256, LAT))
    row = iota((128, 1), 0)
    notes = pick(one_hot(row // 8 * 8 + 5, 128), got[:, 0:128])
    lane = iota((128, 128), 1)
    want = jnp.sum(jnp.where(lane == row % 8, notes, 0.0), axis=1, keepdims=True).astype(i32)
    want = jnp.where(row % 8 < 2, want, -1)
    rope = pick(one_hot(want, 32), rope_ref[...])
    row = iota((8, 1), 0)
    source = jnp.where(row == 2, 4, jnp.where(row >= 4, row - 4, -1))
    hot = pick(one_hot(hot_ref[0] * 8 + source, 128) * (source >= 0).astype(bf16), got)
    for z in range(16):
        out_ref[z, 0:16, :] = lat[z * 16 : z * 16 + 16].astype(bf16)
        out_ref[z, 16:24, :] = (rope[z * 8 : z * 8 + 8] + hot).astype(bf16)


def share_kernel(owners_ref, got_ref, out_ref):
    row = iota((256, 1), 0)
    slot, token = row % 32, row // 32
    index = (slot - COLD) * (2 * PACK) + token // 4 * PACK + 20 + token % 4
    rope_slot = iota((32, 1), 0)
    rope_index = (rope_slot - COLD) * (2 * PACK) + 18
    for i in range(COLD):
        owner = owners_ref[i]
        at, side = owner // 2 * PACK, owner % 2
        index = jnp.where(slot == i, at + side * SHARE + token, index)
        rope_index = jnp.where(rope_slot == i, at + 16 + side, rope_index)
    lat = one_hot(index, 16 * PACK)
    rope = one_hot(rope_index, 16 * PACK)
    table = got_ref[...].reshape(16 * PACK, LAT)
    lat = pick(lat, table).astype(bf16)
    rope = pick(rope, table).astype(bf16)
    for n in range(4):
        out_ref[n, 0:256, :] = lat
        out_ref[n, 256:ROWS, :] = rope


def layout_kernel(q_ref, out_ref):
    for h in range(HEADS):
        base = HEADS * LAT + h * ROPE
        rows = pl.ds(h * QB, QB)
        part = q_ref[:, base : base + ROPE]
        out_ref[rows, 0:LAT] = q_ref[:, h * LAT : (h + 1) * LAT]
        out_ref[rows, LAT:WIDE] = jnp.concatenate([part, part], axis=1)


def attend(q_ref, ref, places):
    lane = iota((32, 2 * ROPE), 1)
    scores = []
    for n in range(4):
        for t in range(SHARE):
            pair = ref[n, 256:ROWS, t // 2 * 128 : t // 2 * 128 + 128]
            own = lane < ROPE if t % 2 == 0 else lane >= ROPE
            places[n, t * 32 : t * 32 + 32, :] = jnp.where(own, pair, 0)
        keys = jnp.concatenate([ref[n, 0:256, :], places[n]], axis=1)
        scores.append(
            lax.dot_general(
                q_ref[...], keys, (((1,), (1,)), ((), ())), preferred_element_type=f32
            )
        )
    top = jnp.maximum(jnp.maximum(scores[0], scores[1]), jnp.maximum(scores[2], scores[3]))
    top = jnp.max(top, axis=1, keepdims=True) * (SCORE_SCALE * LOG2E)
    total = jnp.zeros((HEADS * QB, 256), f32)
    blended = jnp.zeros((HEADS * QB, LAT), f32)
    for n, s in enumerate(scores):
        p = jnp.exp2(s * (SCORE_SCALE * LOG2E) - top)
        total = total + p
        blended = blended + jnp.dot(p.astype(bf16), ref[n, 0:256, :], preferred_element_type=f32)
    return top, jnp.sum(total, axis=1, keepdims=True), blended


def first_half_kernel(
    q0_ref, q1_ref, mine_ref, blend0_ref, stat0_ref, blend1_ref, stat1_ref, places
):
    outs = ((q0_ref, blend0_ref, stat0_ref), (q1_ref, blend1_ref, stat1_ref))
    for q_ref, blend_ref, stat_ref in outs:
        top, total, blended = attend(q_ref, mine_ref, places)
        blend_ref[...] = blended
        stat_ref[:, 0:128] = jnp.broadcast_to(top, (HEADS * QB, 128))
        stat_ref[:, 128:256] = jnp.broadcast_to(total, (HEADS * QB, 128))


def second_half_kernel(q_ref, other_ref, blend_ref, stat_ref, w_ref, o_ref, places):
    top, total, blended = attend(q_ref, other_ref, places)
    top0, total0 = stat_ref[:, 0:1], stat_ref[:, 128:129]
    both = jnp.maximum(top, top0)
    mine, other = jnp.exp2(top0 - both), jnp.exp2(top - both)
    scale = 1.0 / (total0 * mine + total * other)
    latent = (blend_ref[...] * (mine * scale) + blended * (other * scale)).astype(bf16)
    for h in range(HEADS):
        o_ref[:, h * VH : (h + 1) * VH] = jnp.dot(
            latent[h * QB : (h + 1) * QB], w_ref[h], preferred_element_type=f32
        ).astype(bf16)


def local(q_latent, q_rope, kv_latent, k_rope, selection, w_uv):
    z, k, y, x = (lax.axis_index(a) for a in ("z", "core", "y", "x"))
    vmem = pl.BlockSpec(memory_space=pltpu.VMEM)
    smem = pl.BlockSpec(memory_space=pltpu.SMEM)
    params = pltpu.CompilerParams(vmem_limit_bytes=12 * 1024 * 1024)
    swap = [(0, 1), (1, 0)]

    lat = lax.dynamic_slice_in_dim(kv_latent, y * 16, 16, 1)
    rope = lax.dynamic_slice_in_dim(k_rope, y * 1024, 1024, 1)
    hot_first = jnp.max(selection[:, 0])
    cold = selection[:, HOT:]
    notes = jnp.concatenate([cold >> 4, cold & 15], axis=1).astype(bf16)
    notes = jnp.pad(notes, ((0, 6), (0, LAT - 2 * COLD)))
    theirs = jnp.concatenate(
        [
            lax.dynamic_slice_in_dim(lat, (1 - k) * SHARE, SHARE, 1).reshape(128, LAT),
            lax.dynamic_slice_in_dim(rope, (1 - k) * LAT, LAT, 1),
            notes,
        ],
        axis=0,
    )
    swapped = lax.ppermute(theirs, "core", swap)
    own = lax.dynamic_slice_in_dim(lat, k * SHARE, SHARE, 1)
    other = swapped[:128].reshape(16, SHARE, LAT)
    lat = jnp.where(k == 0, jnp.concatenate([own, other]), jnp.concatenate([other, own]))
    own, other = lax.dynamic_slice_in_dim(rope, k * LAT, LAT, 1), swapped[128:144]
    rope = jnp.where(k == 0, jnp.concatenate([own, other]), jnp.concatenate([other, own]))
    notes = jnp.where(x // 2 == k, notes, swapped[144:])
    notes = jnp.where(x % 2 == 0, notes[0, : 2 * COLD], notes[1, : 2 * COLD]).astype(i32)
    owners, places = notes[:COLD], notes[COLD:]

    match = owners[None, :] == jnp.arange(32)[:, None]
    wants = jnp.sum(jnp.where(match, places[None, :], 0), axis=1).reshape(16, 2)
    wants = wants + jnp.arange(2)[None, :] * 16
    hot = lax.dynamic_slice_in_dim(lat, hot_first & 31, HOT, 0).reshape(16, 4, LAT)
    hot_rope = lax.dynamic_slice_in_dim(rope, hot_first & 31, HOT, 0)
    hot_rope = jnp.broadcast_to(hot_rope[:, None, None, :], (HOT, 2, 1, LAT)).reshape(16, 1, LAT)
    wants = jnp.pad(wants.astype(bf16)[:, None, :], ((0, 0), (0, 2), (0, LAT - 2)))
    first = jnp.concatenate([hot, hot_rope, wants], axis=1)
    first, w_uv, q_latent, q_rope = lax.optimization_barrier((first, w_uv, q_latent, q_rope))
    first = lax.all_to_all(first, "z", split_axis=0, concat_axis=0, tiled=True)

    def pairs(r):
        return [
            (c * 4 + s, (s // 2) * 4 + 2 * c + (s + r) % 2) for c in range(2) for s in range(4)
        ]

    queries = []
    for r in range(2):
        m = (x + r) % 2
        part = jnp.concatenate(
            [
                lax.dynamic_slice_in_dim(q_latent, m * QB, QB, 0),
                lax.dynamic_slice_in_dim(q_rope, m * QB, QB, 0),
            ],
            axis=1,
        )
        queries.append(part)

    def travel(r):
        return pl.pallas_call(
            layout_kernel,
            out_shape=jax.ShapeDtypeStruct((HEADS * QB, WIDE), bf16),
            in_specs=[vmem],
            out_specs=vmem,
            compiler_params=params,
        )(lax.ppermute(queries[r], ("core", "x"), pairs(r)))

    ups = [lax.ppermute(w_uv, ("core", "x"), pairs(r)) for r in range(2)]

    second = pl.pallas_call(
        send_kernel,
        out_shape=jax.ShapeDtypeStruct((16, PACK, LAT), bf16),
        in_specs=[smem, vmem, vmem, vmem],
        out_specs=vmem,
        compiler_params=params,
        cost_estimate=pl.CostEstimate(flops=5000000000, bytes_accessed=0, transcendentals=0),
    )((hot_first >> 5)[None], first, lat, rope)
    second, queries[0] = lax.optimization_barrier((second, travel(0)))
    second = lax.all_to_all(second, "z", split_axis=0, concat_axis=0, tiled=True)

    keys = pl.pallas_call(
        share_kernel,
        out_shape=jax.ShapeDtypeStruct((4, ROWS, LAT), bf16),
        in_specs=[smem, vmem],
        out_specs=vmem,
        compiler_params=params,
    )(owners, second)
    keys, queries[1] = lax.optimization_barrier((keys, queries[1]))
    queries[1] = travel(1)
    mine = lax.all_to_all(keys, "y", split_axis=0, concat_axis=0, tiled=True)
    mine, queries, ups = lax.optimization_barrier((mine, queries, ups))
    other = lax.ppermute(mine, "core", swap)

    rows = HEADS * QB
    blend = jax.ShapeDtypeStruct((rows, LAT), f32)
    stat = jax.ShapeDtypeStruct((rows, 256), f32)
    scratch = [pltpu.VMEM((4, 256, 2 * ROPE), bf16)]
    halves = pl.pallas_call(
        first_half_kernel,
        out_shape=[blend, stat, blend, stat],
        in_specs=[vmem] * 3,
        out_specs=[vmem] * 4,
        scratch_shapes=scratch,
        compiler_params=params,
    )(queries[0], queries[1], mine)
    outs = []
    for r in range(2):
        out = pl.pallas_call(
            second_half_kernel,
            out_shape=jax.ShapeDtypeStruct((QB, HEADS * VH), bf16),
            in_specs=[vmem] * 5,
            out_specs=vmem,
            scratch_shapes=scratch,
            compiler_params=params,
        )(queries[r], other, halves[2 * r], halves[2 * r + 1], ups[r])
        outs.append(lax.ppermute(out, ("core", "x"), [(d, s) for s, d in pairs(r)]))
    even = x % 2 == 0
    return jnp.concatenate(
        [jnp.where(even, outs[0], outs[1]), jnp.where(even, outs[1], outs[0])], axis=0
    )


def solution(mesh):
    grid = Mesh(mesh.devices.reshape(16, 2, 4, 4), ("z", "core", "y", "x"))
    ctx, head = ("z", "core"), ("y", "x")
    in_specs = (
        P(ctx, head),
        P(ctx, head),
        P(ctx, None, None),
        P(ctx, None),
        P(ctx, None),
        P(head, None, None),
    )
    return jax.shard_map(
        local, mesh=grid, in_specs=in_specs, out_specs=P(ctx, head), check_vma=False
    )
```

```python
import jax
import jax.numpy as jnp
from jax import lax
from jax.experimental import pallas as pl
from jax.experimental.pallas import tpu as pltpu
from jax.sharding import Mesh
from jax.sharding import PartitionSpec as P

LAT = 512
ROPE = 64
VH = 128
HOT = 8
COLD = 24
WIDE = LAT + 2 * ROPE
SHARE = 8
QB = 64
HEADS = 8
NOTE = 24
PACK = 24
ROWS = 288

SCORE_SCALE = 192.0 ** (-0.5)
LOG2E = 1.4426950408889634

bf16 = jnp.bfloat16
f32 = jnp.float32
i32 = jnp.int32


def iota(shape, axis):
    return lax.broadcasted_iota(i32, shape, axis)


def one_hot(index, width):
    return jnp.where(index == iota((index.shape[0], width), 1), 1.0, 0.0).astype(bf16)


def pick(selector, rows):
    return jnp.dot(selector, rows, preferred_element_type=f32)


def read_kernel(selection_ref, kv_ref, rope_ref, own_ref, theirs_ref, lat, rope, sems):
    y, k = lax.axis_index("y"), lax.axis_index("core")
    tokens = pl.ds(pl.multiple_of(y * 16, 16), 16)
    columns = pl.ds(pl.multiple_of(y * 1024, 1024), 1024)
    copies = [
        pltpu.make_async_copy(kv_ref.at[:, tokens, :], lat, sems.at[0]),
        pltpu.make_async_copy(rope_ref.at[:, columns], rope, sems.at[1]),
    ]
    for copy in copies:
        copy.start()
    row = iota((8, 32), 0)
    one, two = selection_ref[0:1, :], selection_ref[1:2, :]
    notes = jnp.where(row % 2 == 0, one, two)
    notes = jnp.where(row < 2, notes >> 4, jnp.where(row < 4, notes & 15, 0))
    notes = jnp.concatenate([notes.astype(f32), jnp.zeros((8, LAT - 32), f32)], axis=1)
    for ref in (own_ref, theirs_ref):
        ref[144:152, :] = notes.astype(bf16)
    for copy in copies:
        copy.wait()
    low, high = lat[:, 0:8, :].reshape(128, LAT), lat[:, 8:16, :].reshape(128, LAT)
    own_ref[0:128, :] = jnp.where(k == 0, low, high)
    theirs_ref[0:128, :] = jnp.where(k == 0, high, low)
    low, high = rope[:, 0:LAT], rope[:, LAT:]
    own_ref[128:144, :] = jnp.where(k == 0, low, high)
    theirs_ref[128:144, :] = jnp.where(k == 0, high, low)


def join_kernel(selection_ref, own_ref, other_ref, lat_ref, rope_ref, first_ref, owners_ref):
    k, x = lax.axis_index("core"), lax.axis_index("x")
    hot = selection_ref[0:1, 0:1] & 31
    own, other = own_ref[...], other_ref[...]
    one, two = jnp.where(k == 0, own, other), jnp.where(k == 0, other, own)
    lat_ref[0:128, :], lat_ref[128:256, :] = one[0:128], two[0:128]
    rope_ref[0:16, :], rope_ref[16:32, :] = one[128:144], two[128:144]
    notes = jnp.where(x // 2 == k, own[144:152, 0:128], other[144:152, 0:128]).astype(f32)
    owner = jnp.where(x % 2 == 0, notes[0:1], notes[1:2])
    place = jnp.where(x % 2 == 0, notes[2:3], notes[3:4])
    owners_ref[...] = jnp.broadcast_to(owner, (8, 128)).astype(i32)
    count = 16 * NOTE
    lane, row = iota((count, 128), 1), iota((count, 1), 0)
    z, part = row // NOTE, row % NOTE
    cold = (lane >= HOT) & (lane < HOT + COLD)
    rows = jnp.zeros((count, 128), f32)
    for c in range(2):
        match = cold & (owner.astype(i32) == z * 2 + c) & (part == 18)
        want = jnp.sum(jnp.where(match, place, 0.0), axis=1, keepdims=True) + c * 16
        rows = jnp.where((part == 18) & (lane == c), want, rows)
    for c in range(4):
        chosen = (part < 16) & (part % 4 == c)
        index = jnp.where(chosen, hot * 8 + z * 4 + part // 4, -1)
        rows = rows + pick(one_hot(index, 256), lat_ref[:, c * 128 : c * 128 + 128])
        index = jnp.where(z % 2 * 2 + part - 16 == c, hot + z // 2, -1)
        index = jnp.where((part == 16) | (part == 17), index, -1)
        rows = rows + pick(one_hot(index, 32), rope_ref[:, c * 128 : c * 128 + 128])
    first_ref[...] = rows.astype(bf16)


def send_kernel(selection_ref, first_ref, lat_ref, rope_ref, out_ref):
    got = first_ref[...]
    row = iota((256, 1), 0)
    notes = pick(one_hot(row // 16 * NOTE + 18, 16 * NOTE), got)
    lane = iota((256, 128), 1)
    want = jnp.sum(jnp.where(lane == row // 8 % 2, notes, 0.0), axis=1, keepdims=True)
    lat = pick(one_hot(want.astype(i32) * 8 + row % 8, 256), lat_ref[...])
    row = iota((128, 1), 0)
    notes = pick(one_hot(row // 8 * NOTE + 18, 16 * NOTE), got)
    lane = iota((128, 128), 1)
    want = jnp.sum(jnp.where(lane == row % 8, notes, 0.0), axis=1, keepdims=True).astype(i32)
    want = jnp.where(row % 8 < 2, want, -1)
    rope = pick(one_hot(want, 32), rope_ref[...])
    row = iota((8, 1), 0)
    holder = (selection_ref[0:1, 0:1] >> 5) * NOTE
    half = lax.axis_index("z") % 2
    hot = []
    for c in range(4):
        index = jnp.where(row >= 4, holder + (row - 4) * 4 + c, -1)
        index = jnp.where((row == 2) & (half == c // 2), holder + 16 + c % 2, index)
        hot.append(pick(one_hot(index, 16 * NOTE), got))
    hot = jnp.concatenate(hot, axis=1)
    for z in range(16):
        out_ref[z, 0:16, :] = lat[z * 16 : z * 16 + 16].astype(bf16)
        out_ref[z, 16:24, :] = (rope[z * 8 : z * 8 + 8] + hot).astype(bf16)


def share_kernel(owners_ref, got_ref, out_ref):
    row = iota((256, 1), 0)
    slot, token = row % 32, row // 32
    index = (slot - COLD) * (2 * PACK) + token // 4 * PACK + 20 + token % 4
    rope_slot = iota((32, 1), 0)
    rope_index = (rope_slot - COLD) * (2 * PACK) + 18
    for i in range(COLD):
        owner = owners_ref[i]
        at, side = owner // 2 * PACK, owner % 2
        index = jnp.where(slot == i, at + side * SHARE + token, index)
        rope_index = jnp.where(rope_slot == i, at + 16 + side, rope_index)
    lat = one_hot(index, 16 * PACK)
    rope = one_hot(rope_index, 16 * PACK)
    rope = rope + one_hot(jnp.where(rope_slot >= COLD, rope_index + PACK, -1), 16 * PACK)
    table = got_ref[...].reshape(16 * PACK, LAT)
    lat = pick(lat, table).astype(bf16)
    rope = pick(rope, table).astype(bf16)
    for n in range(4):
        out_ref[n, 0:256, :] = lat
        out_ref[n, 256:ROWS, :] = rope


def layout_kernel(q_ref, out_ref):
    for h in range(HEADS):
        base = HEADS * LAT + h * ROPE
        rows = pl.ds(h * QB, QB)
        part = q_ref[:, base : base + ROPE]
        out_ref[rows, 0:LAT] = q_ref[:, h * LAT : (h + 1) * LAT]
        out_ref[rows, LAT:WIDE] = jnp.concatenate([part, part], axis=1)


def attend(q_ref, ref, places):
    lane = iota((32, 2 * ROPE), 1)
    scores = []
    for n in range(4):
        for t in range(SHARE):
            pair = ref[n, 256:ROWS, t // 2 * 128 : t // 2 * 128 + 128]
            own = lane < ROPE if t % 2 == 0 else lane >= ROPE
            places[n, t * 32 : t * 32 + 32, :] = jnp.where(own, pair, 0)
        keys = jnp.concatenate([ref[n, 0:256, :], places[n]], axis=1)
        scores.append(
            lax.dot_general(
                q_ref[...], keys, (((1,), (1,)), ((), ())), preferred_element_type=f32
            )
        )
    top = jnp.maximum(jnp.maximum(scores[0], scores[1]), jnp.maximum(scores[2], scores[3]))
    top = jnp.max(top, axis=1, keepdims=True) * (SCORE_SCALE * LOG2E)
    total = jnp.zeros((HEADS * QB, 256), f32)
    blended = jnp.zeros((HEADS * QB, LAT), f32)
    for n, s in enumerate(scores):
        p = jnp.exp2(s * (SCORE_SCALE * LOG2E) - top)
        total = total + p
        blended = blended + jnp.dot(p.astype(bf16), ref[n, 0:256, :], preferred_element_type=f32)
    return top, jnp.sum(total, axis=1, keepdims=True), blended


def first_half_kernel(
    q0_ref, q1_ref, mine_ref, blend0_ref, stat0_ref, blend1_ref, stat1_ref, places
):
    outs = ((q0_ref, blend0_ref, stat0_ref), (q1_ref, blend1_ref, stat1_ref))
    for q_ref, blend_ref, stat_ref in outs:
        top, total, blended = attend(q_ref, mine_ref, places)
        blend_ref[...] = blended
        stat_ref[:, 0:128] = jnp.broadcast_to(top, (HEADS * QB, 128))
        stat_ref[:, 128:256] = jnp.broadcast_to(total, (HEADS * QB, 128))


def second_half_kernel(q_ref, other_ref, blend_ref, stat_ref, w_ref, o_ref, places, w, sem):
    up = pltpu.make_async_copy(w_ref, w, sem)
    up.start()
    top, total, blended = attend(q_ref, other_ref, places)
    top0, total0 = stat_ref[:, 0:1], stat_ref[:, 128:129]
    both = jnp.maximum(top, top0)
    mine, other = jnp.exp2(top0 - both), jnp.exp2(top - both)
    scale = 1.0 / (total0 * mine + total * other)
    latent = (blend_ref[...] * (mine * scale) + blended * (other * scale)).astype(bf16)
    up.wait()
    for h in range(HEADS):
        o_ref[:, h * VH : (h + 1) * VH] = jnp.dot(
            latent[h * QB : (h + 1) * QB], w[h], preferred_element_type=f32
        ).astype(bf16)


def local(q_latent, q_rope, kv_latent, k_rope, selection, w_uv):
    z, k, y, x = (lax.axis_index(a) for a in ("z", "core", "y", "x"))
    vmem = pl.BlockSpec(memory_space=pltpu.VMEM)
    smem = pl.BlockSpec(memory_space=pltpu.SMEM)
    params = pltpu.CompilerParams(vmem_limit_bytes=12 * 1024 * 1024)
    anywhere = pl.BlockSpec(memory_space=pl.ANY)
    swap = [(0, 1), (1, 0)]

    pack = jax.ShapeDtypeStruct((152, LAT), bf16)
    own, theirs = pl.pallas_call(
        read_kernel,
        out_shape=[pack, pack],
        in_specs=[vmem, anywhere, anywhere],
        out_specs=[vmem, vmem],
        scratch_shapes=[
            pltpu.VMEM((16, 16, LAT), bf16),
            pltpu.VMEM((16, 2 * LAT), bf16),
            pltpu.SemaphoreType.DMA((2,)),
        ],
        compiler_params=params,
    )(selection, kv_latent, k_rope)
    swapped = lax.ppermute(theirs, "core", swap)

    lat, rope, first, owners = pl.pallas_call(
        join_kernel,
        out_shape=[
            jax.ShapeDtypeStruct((256, LAT), bf16),
            jax.ShapeDtypeStruct((32, LAT), bf16),
            jax.ShapeDtypeStruct((16 * NOTE, 128), bf16),
            jax.ShapeDtypeStruct((8, 128), i32),
        ],
        in_specs=[vmem] * 3,
        out_specs=[vmem] * 4,
        compiler_params=params,
    )(selection, own, swapped)
    owners = owners[0, HOT : HOT + COLD]
    first, w_uv, q_latent, q_rope = lax.optimization_barrier((first, w_uv, q_latent, q_rope))
    first = first.reshape(16, NOTE, 128)
    first = lax.all_to_all(first, "z", split_axis=0, concat_axis=0, tiled=True)
    first = first.reshape(16 * NOTE, 128)

    def pairs(r):
        return [
            (c * 4 + s, (s // 2) * 4 + 2 * c + (s + r) % 2) for c in range(2) for s in range(4)
        ]

    queries = []
    for r in range(2):
        m = (x + r) % 2
        part = jnp.concatenate(
            [
                lax.dynamic_slice_in_dim(q_latent, m * QB, QB, 0),
                lax.dynamic_slice_in_dim(q_rope, m * QB, QB, 0),
            ],
            axis=1,
        )
        queries.append(part)

    def travel(r):
        return pl.pallas_call(
            layout_kernel,
            out_shape=jax.ShapeDtypeStruct((HEADS * QB, WIDE), bf16),
            in_specs=[vmem],
            out_specs=vmem,
            compiler_params=params,
        )(lax.ppermute(queries[r], ("core", "x"), pairs(r)))

    ups = [lax.ppermute(w_uv, ("core", "x"), pairs(r)) for r in range(2)]

    second = pl.pallas_call(
        send_kernel,
        out_shape=jax.ShapeDtypeStruct((16, PACK, LAT), bf16),
        in_specs=[vmem] * 4,
        out_specs=vmem,
        compiler_params=params,
        cost_estimate=pl.CostEstimate(flops=5000000000, bytes_accessed=0, transcendentals=0),
    )(selection, first, lat, rope)
    second, queries[0] = lax.optimization_barrier((second, travel(0)))
    second = lax.all_to_all(second, "z", split_axis=0, concat_axis=0, tiled=True)

    keys = pl.pallas_call(
        share_kernel,
        out_shape=jax.ShapeDtypeStruct((4, ROWS, LAT), bf16),
        in_specs=[smem, vmem],
        out_specs=vmem,
        compiler_params=params,
    )(owners, second)
    keys, queries[1] = lax.optimization_barrier((keys, queries[1]))
    queries[1] = travel(1)
    mine = lax.all_to_all(keys, "y", split_axis=0, concat_axis=0, tiled=True)
    mine, queries, ups = lax.optimization_barrier((mine, queries, ups))
    other = lax.ppermute(mine, "core", swap)

    rows = HEADS * QB
    blend = jax.ShapeDtypeStruct((rows, LAT), f32)
    stat = jax.ShapeDtypeStruct((rows, 256), f32)
    scratch = [pltpu.VMEM((4, 256, 2 * ROPE), bf16)]
    halves = pl.pallas_call(
        first_half_kernel,
        out_shape=[blend, stat, blend, stat],
        in_specs=[vmem] * 3,
        out_specs=[vmem] * 4,
        scratch_shapes=scratch,
        compiler_params=params,
    )(queries[0], queries[1], mine)
    outs = []
    for r in range(2):
        out = pl.pallas_call(
            second_half_kernel,
            out_shape=jax.ShapeDtypeStruct((QB, HEADS * VH), bf16),
            in_specs=[vmem] * 4 + [anywhere],
            out_specs=vmem,
            scratch_shapes=scratch
            + [pltpu.VMEM((HEADS, LAT, VH), bf16), pltpu.SemaphoreType.DMA],
            compiler_params=params,
        )(queries[r], other, halves[2 * r], halves[2 * r + 1], ups[r])
        outs.append(lax.ppermute(out, ("core", "x"), [(d, s) for s, d in pairs(r)]))
    even = x % 2 == 0
    return jnp.concatenate(
        [jnp.where(even, outs[0], outs[1]), jnp.where(even, outs[1], outs[0])], axis=0
    )


def solution(mesh):
    grid = Mesh(mesh.devices.reshape(16, 2, 4, 4), ("z", "core", "y", "x"))
    ctx, head = ("z", "core"), ("y", "x")
    in_specs = (
        P(ctx, head),
        P(ctx, head),
        P(ctx, None, None),
        P(ctx, None),
        P(ctx, None),
        P(head, None, None),
    )
    return jax.shard_map(
        local, mesh=grid, in_specs=in_specs, out_specs=P(ctx, head), check_vma=False
    )
```

```python
import jax
import jax.numpy as jnp
from jax import lax
from jax.experimental import pallas as pl
from jax.experimental.pallas import tpu as pltpu
from jax.sharding import Mesh
from jax.sharding import PartitionSpec as P

LAT = 512
ROPE = 64
VH = 128
HOT = 8
COLD = 24
WIDE = LAT + 2 * ROPE
SHARE = 8
QB = 64
HEADS = 8
NOTE = 24
PACK = 24
ROWS = 288

SCORE_SCALE = 192.0 ** (-0.5)
LOG2E = 1.4426950408889634

bf16 = jnp.bfloat16
f32 = jnp.float32
i32 = jnp.int32


def iota(shape, axis):
    return lax.broadcasted_iota(i32, shape, axis)


def one_hot(index, width):
    return jnp.where(index == iota((index.shape[0], width), 1), 1.0, 0.0).astype(bf16)


def pick(selector, rows):
    return jnp.dot(selector, rows, preferred_element_type=f32)


def read_kernel(selection_ref, kv_ref, rope_ref, own_ref, theirs_ref, lat, rope, sems):
    y, k = lax.axis_index("y"), lax.axis_index("core")
    tokens = pl.ds(pl.multiple_of(y * 16, 16), 16)
    columns = pl.ds(pl.multiple_of(y * 1024, 1024), 1024)
    copies = [
        pltpu.make_async_copy(kv_ref.at[:, tokens, :], lat, sems.at[0]),
        pltpu.make_async_copy(rope_ref.at[:, columns], rope, sems.at[1]),
    ]
    for copy in copies:
        copy.start()
    row = iota((8, 32), 0)
    one, two = selection_ref[0:1, :], selection_ref[1:2, :]
    notes = jnp.where(row % 2 == 0, one, two)
    notes = jnp.where(row < 2, notes >> 4, jnp.where(row < 4, notes & 15, 0))
    notes = jnp.concatenate([notes.astype(f32), jnp.zeros((8, LAT - 32), f32)], axis=1)
    for ref in (own_ref, theirs_ref):
        ref[144:152, :] = notes.astype(bf16)
    for copy in copies:
        copy.wait()
    low, high = lat[:, 0:8, :].reshape(128, LAT), lat[:, 8:16, :].reshape(128, LAT)
    own_ref[0:128, :] = jnp.where(k == 0, low, high)
    theirs_ref[0:128, :] = jnp.where(k == 0, high, low)
    low, high = rope[:, 0:LAT], rope[:, LAT:]
    own_ref[128:144, :] = jnp.where(k == 0, low, high)
    theirs_ref[128:144, :] = jnp.where(k == 0, high, low)


def join_kernel(selection_ref, own_ref, other_ref, lat_ref, rope_ref, first_ref, owners_ref):
    k, x = lax.axis_index("core"), lax.axis_index("x")
    hot = selection_ref[0:1, 0:1] & 31
    own, other = own_ref[...], other_ref[...]
    one, two = jnp.where(k == 0, own, other), jnp.where(k == 0, other, own)
    lat_ref[0:128, :], lat_ref[128:256, :] = one[0:128], two[0:128]
    rope_ref[0:16, :], rope_ref[16:32, :] = one[128:144], two[128:144]
    notes = jnp.where(x // 2 == k, own[144:152, 0:128], other[144:152, 0:128]).astype(f32)
    owner = jnp.where(x % 2 == 0, notes[0:1], notes[1:2])
    place = jnp.where(x % 2 == 0, notes[2:3], notes[3:4])
    owners_ref[...] = jnp.broadcast_to(owner, (8, 128)).astype(i32)
    count = 16 * NOTE
    lane, row = iota((count, 128), 1), iota((count, 1), 0)
    z, part = row // NOTE, row % NOTE
    cold = (lane >= HOT) & (lane < HOT + COLD)
    rows = jnp.zeros((count, 128), f32)
    for c in range(2):
        match = cold & (owner.astype(i32) == z * 2 + c) & (part == 18)
        want = jnp.sum(jnp.where(match, place, 0.0), axis=1, keepdims=True) + c * 16
        rows = jnp.where((part == 18) & (lane == c), want, rows)
    tokens = pick(one_hot(hot * 8 + iota((64, 1), 0), 256), lat_ref[...]).astype(bf16)
    places = pick(one_hot(hot + iota((16, 1), 0), 32), rope_ref[...]).astype(bf16)
    for c in range(4):
        index = jnp.where((part < 16) & (part % 4 == c), z * 4 + part // 4, -1)
        rows = rows + pick(one_hot(index, 64), tokens[:, c * 128 : c * 128 + 128])
        index = jnp.where(z % 2 * 2 + part - 16 == c, z // 2, -1)
        index = jnp.where((part == 16) | (part == 17), index, -1)
        rows = rows + pick(one_hot(index, 16), places[:, c * 128 : c * 128 + 128])
    first_ref[...] = rows.astype(bf16)


def send_kernel(selection_ref, first_ref, lat_ref, rope_ref, out_ref):
    got = first_ref[...]
    row = iota((256, 1), 0)
    notes = pick(one_hot(row // 16 * NOTE + 18, 16 * NOTE), got)
    lane = iota((256, 128), 1)
    want = jnp.sum(jnp.where(lane == row // 8 % 2, notes, 0.0), axis=1, keepdims=True)
    lat = pick(one_hot(want.astype(i32) * 8 + row % 8, 256), lat_ref[...])
    row = iota((128, 1), 0)
    notes = pick(one_hot(row // 8 * NOTE + 18, 16 * NOTE), got)
    lane = iota((128, 128), 1)
    want = jnp.sum(jnp.where(lane == row % 8, notes, 0.0), axis=1, keepdims=True).astype(i32)
    want = jnp.where(row % 8 < 2, want, -1)
    rope = pick(one_hot(want, 32), rope_ref[...])
    row = iota((8, 1), 0)
    holder = (selection_ref[0:1, 0:1] >> 5) * NOTE
    half = lax.axis_index("z") % 2
    hot = []
    for c in range(4):
        index = jnp.where(row >= 4, holder + (row - 4) * 4 + c, -1)
        index = jnp.where((row == 2) & (half == c // 2), holder + 16 + c % 2, index)
        hot.append(pick(one_hot(index, 16 * NOTE), got))
    hot = jnp.concatenate(hot, axis=1)
    for z in range(16):
        out_ref[z, 0:16, :] = lat[z * 16 : z * 16 + 16].astype(bf16)
        out_ref[z, 16:24, :] = (rope[z * 8 : z * 8 + 8] + hot).astype(bf16)


def share_kernel(owners_ref, got_ref, out_ref):
    row = iota((256, 1), 0)
    slot, token = row % 32, row // 32
    index = (slot - COLD) * (2 * PACK) + token // 4 * PACK + 20 + token % 4
    rope_slot = iota((32, 1), 0)
    rope_index = (rope_slot - COLD) * (2 * PACK) + 18
    for i in range(COLD):
        owner = owners_ref[i]
        at, side = owner // 2 * PACK, owner % 2
        index = jnp.where(slot == i, at + side * SHARE + token, index)
        rope_index = jnp.where(rope_slot == i, at + 16 + side, rope_index)
    lat = one_hot(index, 16 * PACK)
    rope = one_hot(rope_index, 16 * PACK)
    rope = rope + one_hot(jnp.where(rope_slot >= COLD, rope_index + PACK, -1), 16 * PACK)
    table = got_ref[...].reshape(16 * PACK, LAT)
    lat = pick(lat, table).astype(bf16)
    rope = pick(rope, table).astype(bf16)
    for n in range(4):
        out_ref[n, 0:256, :] = lat
        out_ref[n, 256:ROWS, :] = rope


def layout_kernel(q_ref, out_ref):
    for h in range(HEADS):
        base = HEADS * LAT + h * ROPE
        rows = pl.ds(h * QB, QB)
        part = q_ref[:, base : base + ROPE]
        out_ref[rows, 0:LAT] = q_ref[:, h * LAT : (h + 1) * LAT]
        out_ref[rows, LAT:WIDE] = jnp.concatenate([part, part], axis=1)


def spread(ref, places):
    lane = iota((32, 2 * ROPE), 1)
    for n in range(4):
        for t in range(SHARE):
            pair = ref[n, 256:ROWS, t // 2 * 128 : t // 2 * 128 + 128]
            own = lane < ROPE if t % 2 == 0 else lane >= ROPE
            places[n, t * 32 : t * 32 + 32, :] = jnp.where(own, pair, 0)


def attend(q_ref, ref, places):
    scores = []
    for n in range(4):
        keys = jnp.concatenate([ref[n, 0:256, :], places[n]], axis=1)
        scores.append(
            lax.dot_general(
                q_ref[...], keys, (((1,), (1,)), ((), ())), preferred_element_type=f32
            )
        )
    top = jnp.maximum(jnp.maximum(scores[0], scores[1]), jnp.maximum(scores[2], scores[3]))
    top = jnp.max(top, axis=1, keepdims=True) * (SCORE_SCALE * LOG2E)
    total = jnp.zeros((HEADS * QB, 256), f32)
    blended = jnp.zeros((HEADS * QB, LAT), f32)
    for n, s in enumerate(scores):
        p = jnp.exp2(s * (SCORE_SCALE * LOG2E) - top)
        total = total + p
        blended = blended + jnp.dot(p.astype(bf16), ref[n, 0:256, :], preferred_element_type=f32)
    return top, jnp.sum(total, axis=1, keepdims=True), blended


def first_half_kernel(
    q0_ref, q1_ref, mine_ref, blend0_ref, stat0_ref, blend1_ref, stat1_ref, places
):
    spread(mine_ref, places)
    outs = ((q0_ref, blend0_ref, stat0_ref), (q1_ref, blend1_ref, stat1_ref))
    for q_ref, blend_ref, stat_ref in outs:
        top, total, blended = attend(q_ref, mine_ref, places)
        blend_ref[...] = blended
        stat_ref[:, 0:128] = jnp.broadcast_to(top, (HEADS * QB, 128))
        stat_ref[:, 128:256] = jnp.broadcast_to(total, (HEADS * QB, 128))


def second_half_kernel(q_ref, other_ref, blend_ref, stat_ref, w_ref, o_ref, places, w, sem):
    up = pltpu.make_async_copy(w_ref, w, sem)
    up.start()
    spread(other_ref, places)
    top, total, blended = attend(q_ref, other_ref, places)
    top0, total0 = stat_ref[:, 0:1], stat_ref[:, 128:129]
    both = jnp.maximum(top, top0)
    mine, other = jnp.exp2(top0 - both), jnp.exp2(top - both)
    scale = 1.0 / (total0 * mine + total * other)
    latent = (blend_ref[...] * (mine * scale) + blended * (other * scale)).astype(bf16)
    up.wait()
    for h in range(HEADS):
        o_ref[:, h * VH : (h + 1) * VH] = jnp.dot(
            latent[h * QB : (h + 1) * QB], w[h], preferred_element_type=f32
        ).astype(bf16)


def local(q_latent, q_rope, kv_latent, k_rope, selection, w_uv):
    z, k, y, x = (lax.axis_index(a) for a in ("z", "core", "y", "x"))
    vmem = pl.BlockSpec(memory_space=pltpu.VMEM)
    smem = pl.BlockSpec(memory_space=pltpu.SMEM)
    params = pltpu.CompilerParams(vmem_limit_bytes=12 * 1024 * 1024)
    anywhere = pl.BlockSpec(memory_space=pl.ANY)
    hbm = pl.BlockSpec(memory_space=pltpu.HBM)
    swap = [(0, 1), (1, 0)]

    pack = jax.ShapeDtypeStruct((152, LAT), bf16)
    own, theirs = pl.pallas_call(
        read_kernel,
        out_shape=[pack, pack],
        in_specs=[vmem, hbm, hbm],
        out_specs=[vmem, vmem],
        scratch_shapes=[
            pltpu.VMEM((16, 16, LAT), bf16),
            pltpu.VMEM((16, 2 * LAT), bf16),
            pltpu.SemaphoreType.DMA((2,)),
        ],
        compiler_params=params,
    )(selection, kv_latent, k_rope)
    swapped = lax.ppermute(theirs, "core", swap)

    lat, rope, first, owners = pl.pallas_call(
        join_kernel,
        out_shape=[
            jax.ShapeDtypeStruct((256, LAT), bf16),
            jax.ShapeDtypeStruct((32, LAT), bf16),
            jax.ShapeDtypeStruct((16 * NOTE, 128), bf16),
            jax.ShapeDtypeStruct((8, 128), i32),
        ],
        in_specs=[vmem] * 3,
        out_specs=[vmem] * 4,
        compiler_params=params,
    )(selection, own, swapped)
    owners = owners[0, HOT : HOT + COLD]
    first, w_uv, q_latent, q_rope = lax.optimization_barrier((first, w_uv, q_latent, q_rope))
    first = first.reshape(16, NOTE, 128)
    first = lax.all_to_all(first, "z", split_axis=0, concat_axis=0, tiled=True)
    first = first.reshape(16 * NOTE, 128)

    def pairs(r):
        return [
            (c * 4 + s, (s // 2) * 4 + 2 * c + (s + r) % 2) for c in range(2) for s in range(4)
        ]

    queries = []
    for r in range(2):
        m = (x + r) % 2
        part = jnp.concatenate(
            [
                lax.dynamic_slice_in_dim(q_latent, m * QB, QB, 0),
                lax.dynamic_slice_in_dim(q_rope, m * QB, QB, 0),
            ],
            axis=1,
        )
        queries.append(part)

    def travel(r):
        return pl.pallas_call(
            layout_kernel,
            out_shape=jax.ShapeDtypeStruct((HEADS * QB, WIDE), bf16),
            in_specs=[vmem],
            out_specs=vmem,
            compiler_params=params,
        )(lax.ppermute(queries[r], ("core", "x"), pairs(r)))

    ups = [lax.ppermute(w_uv, ("core", "x"), pairs(r)) for r in range(2)]

    second = pl.pallas_call(
        send_kernel,
        out_shape=jax.ShapeDtypeStruct((16, PACK, LAT), bf16),
        in_specs=[vmem] * 4,
        out_specs=vmem,
        compiler_params=params,
        cost_estimate=pl.CostEstimate(flops=5000000000, bytes_accessed=0, transcendentals=0),
    )(selection, first, lat, rope)
    second, queries[0] = lax.optimization_barrier((second, travel(0)))
    second = lax.all_to_all(second, "z", split_axis=0, concat_axis=0, tiled=True)

    keys = pl.pallas_call(
        share_kernel,
        out_shape=jax.ShapeDtypeStruct((4, ROWS, LAT), bf16),
        in_specs=[smem, vmem],
        out_specs=vmem,
        compiler_params=params,
    )(owners, second)
    keys, queries[1] = lax.optimization_barrier((keys, queries[1]))
    queries[1] = travel(1)
    mine = lax.all_to_all(keys, "y", split_axis=0, concat_axis=0, tiled=True)
    mine, queries, ups = lax.optimization_barrier((mine, queries, ups))
    other = lax.ppermute(mine, "core", swap)

    rows = HEADS * QB
    blend = jax.ShapeDtypeStruct((rows, LAT), f32)
    stat = jax.ShapeDtypeStruct((rows, 256), f32)
    scratch = [pltpu.VMEM((4, 256, 2 * ROPE), bf16)]
    halves = pl.pallas_call(
        first_half_kernel,
        out_shape=[blend, stat, blend, stat],
        in_specs=[vmem] * 3,
        out_specs=[vmem] * 4,
        scratch_shapes=scratch,
        compiler_params=params,
    )(queries[0], queries[1], mine)
    outs = []
    for r in range(2):
        out = pl.pallas_call(
            second_half_kernel,
            out_shape=jax.ShapeDtypeStruct((QB, HEADS * VH), bf16),
            in_specs=[vmem] * 4 + [anywhere],
            out_specs=vmem,
            scratch_shapes=scratch
            + [pltpu.VMEM((HEADS, LAT, VH), bf16), pltpu.SemaphoreType.DMA],
            compiler_params=params,
        )(queries[r], other, halves[2 * r], halves[2 * r + 1], ups[r])
        outs.append(lax.ppermute(out, ("core", "x"), [(d, s) for s, d in pairs(r)]))
    even = x % 2 == 0
    return jnp.concatenate(
        [jnp.where(even, outs[0], outs[1]), jnp.where(even, outs[1], outs[0])], axis=0
    )


def solution(mesh):
    grid = Mesh(mesh.devices.reshape(16, 2, 4, 4), ("z", "core", "y", "x"))
    ctx, head = ("z", "core"), ("y", "x")
    in_specs = (
        P(ctx, head),
        P(ctx, head),
        P(ctx, None, None),
        P(ctx, None),
        P(ctx, None),
        P(head, None, None),
    )
    return jax.shard_map(
        local, mesh=grid, in_specs=in_specs, out_specs=P(ctx, head), check_vma=False
    )
```
